128 devices in a mesh: rows: 16 (over y, z_lo, core), cols: 8 (over z_hi, x).
Axes of the slice: x: 4, y: 4, z: 4 (z_hi: 2, z_lo: 2; z = z_hi * 2 + z_lo), core: 2. Of those that a mesh axis runs over, the one named last changes fastest.
Arguments:
- tokens: bfloat16 [512, 1024, 256], P('rows', 'cols'), may hold values from -6 to 6
- norm_gains: float32 [4, 256], replicated, may hold values from 0.5 to 1.5
- qkv_weight: bfloat16 [2, 256, 768], replicated, may hold values from -10 to 10
- out_weight: bfloat16 [2, 256, 256], replicated, may hold values from -0.375 to 0.375
- up_weight: bfloat16 [2, 256, 1024], replicated, may hold values from -0.375 to 0.375
- down_weight: bfloat16 [2, 1024, 256], replicated, may hold values from -0.1875 to 0.1875
Outputs:
- block_output: bfloat16 [512, 1024, 256], P('rows', 'cols')
The draws below stay inside these ranges and needn't reach their ends.
All inputs are finite; a program needn't handle non-finite values.
Results may differ from the reference program's by a relative error of at most 0.018.
Values may be sent and summed in bfloat16 or wider, within the bound.
A program may use at most 128 MiB of HBM per device.

```python
import math
import jax
import jax.numpy as jnp
from jax import lax

CHANNELS = 256
HEADS = 8
MLP_UNITS = 1024
HEAD_DIM = 32
HEIGHT = 512
BREADTH = 1024


def draw_qkv_weight(key, part):
    key = jax.random.fold_in(key, 7)
    return (jax.random.normal(key, (2, CHANNELS, 3 * CHANNELS), jnp.float32) * CHANNELS ** (-0.5)).astype(jnp.bfloat16)


def steps_of(rng, dims, split, smallest, largest):
    level = 1.0
    for position, parts in split:
        steps = jax.random.uniform(jax.random.fold_in(jax.random.fold_in(rng, 6), position), (parts,), jnp.float32, smallest / len(split), largest / len(split))
        level = level * jnp.repeat(jnp.exp(steps), dims[position] // parts).reshape((-1,) + (1,) * (len(dims) - 1 - position))
    return level


def normal_values(rng, extent, scale, limit, split=(), held_as=jnp.bfloat16):
    entries = jax.random.normal(rng, extent, jnp.float32) * scale
    if len(split) > 0:
        entries = steps_of(rng, extent, split, -0.22, 0.18) * entries
    return jnp.clip(entries, min=-limit, max=limit).astype(held_as)


def setup_inputs(seed: int = 0) -> dict:
    arg_keys = jax.random.split(jax.random.key(seed), 7)
    tokens = normal_values(arg_keys[0], (HEIGHT, BREADTH, CHANNELS), 1.0, 6.0, ((0, 16), (1, 8)))
    norm_gains = jnp.clip(1.0 + 0.1 * jax.random.normal(arg_keys[1], (4, CHANNELS), jnp.float32), 0.5, 1.5)
    qkv_weight = draw_qkv_weight(jax.random.fold_in(arg_keys[6], 71), 0)
    out_weight = normal_values(arg_keys[3], (2, CHANNELS, CHANNELS), CHANNELS ** -0.5, 0.375)
    up_weight = normal_values(arg_keys[4], (2, CHANNELS, MLP_UNITS), CHANNELS ** -0.5, 0.375)
    down_weight = normal_values(arg_keys[5], (2, MLP_UNITS, CHANNELS), MLP_UNITS ** -0.5, 0.1875)
    return {"tokens": tokens, "norm_gains": norm_gains, "qkv_weight": qkv_weight, "out_weight": out_weight, "up_weight": up_weight, "down_weight": down_weight}


EPSILON = 1e-06

def layer_norm(raster, norm_gain):
    raster = raster.astype(jnp.float32)
    centred = raster - lax.optimization_barrier(jnp.mean(raster, axis=-1, keepdims=True))
    spread = lax.optimization_barrier(jnp.mean(centred * centred, axis=-1, keepdims=True))
    return (centred * lax.rsqrt(spread + EPSILON) * norm_gain).astype(jnp.bfloat16)

def attend_heads(qkv_heads):
    count, members, _ = qkv_heads.shape
    query_heads = qkv_heads[..., :CHANNELS].astype(jnp.float32).reshape(count, members, HEADS, HEAD_DIM)
    key_heads = qkv_heads[..., CHANNELS:2 * CHANNELS].astype(jnp.float32).reshape(count, members, HEADS, HEAD_DIM)
    value_heads = qkv_heads[..., 2 * CHANNELS:].astype(jnp.float32).reshape(count, members, HEADS, HEAD_DIM)
    scores = jnp.einsum('gqhd,gkhd->ghqk', query_heads, key_heads) / math.sqrt(HEAD_DIM)
    weights = jax.nn.softmax(scores, axis=-1).astype(jnp.bfloat16)
    attended = jnp.einsum('ghqk,gkhd->gqhd', weights.astype(jnp.float32), value_heads)
    return attended.astype(jnp.bfloat16).reshape(count, members, CHANNELS)

def window_split(raster, feature):
    return raster.reshape(HEIGHT // 8, 8, BREADTH // 8, 8, feature).transpose(0, 2, 1, 3, 4).reshape(HEIGHT // 8, BREADTH // 8, 64, feature)

def window_join(groups, feature):
    return groups.reshape(HEIGHT // 8, BREADTH // 8, 8, 8, feature).transpose(0, 2, 1, 3, 4).reshape(HEIGHT, BREADTH, feature)

def grid_split(raster, feature):
    return raster.reshape(8, HEIGHT // 8, 8, BREADTH // 8, feature).transpose(1, 3, 0, 2, 4).reshape(HEIGHT // 8, BREADTH // 8, 64, feature)

def grid_join(groups, feature):
    return groups.reshape(HEIGHT // 8, BREADTH // 8, 8, 8, feature).transpose(2, 0, 3, 1, 4).reshape(HEIGHT, BREADTH, feature)

def attention_terms(groups, norm_gain, weight_in, weight_out):

    def one_band(band_groups):
        normed = layer_norm(band_groups, norm_gain)
        qkv_heads = jnp.dot(normed.reshape(-1, CHANNELS), weight_in, preferred_element_type=jnp.float32).astype(jnp.bfloat16)
        attended = attend_heads(qkv_heads.reshape(band_groups.shape[0], 64, 3 * CHANNELS))
        return jnp.dot(attended.reshape(-1, CHANNELS), weight_out, preferred_element_type=jnp.float32).reshape(band_groups.shape)
    return lax.map(one_band, groups)

def feed_forward(raster, norm_gain, weight_in, weight_out):

    def one_row(raster_row):
        normed = layer_norm(raster_row, norm_gain)
        hidden_units = jax.nn.gelu(jnp.dot(normed, weight_in, preferred_element_type=jnp.float32), approximate=False).astype(jnp.bfloat16)
        return (raster_row.astype(jnp.float32) + jnp.dot(hidden_units, weight_out, preferred_element_type=jnp.float32)).astype(jnp.bfloat16)
    return lax.map(one_row, raster)

def reference(tokens, norm_gains, qkv_weight, out_weight, up_weight, down_weight):
    window_terms = attention_terms(window_split(tokens, CHANNELS), norm_gains[0], qkv_weight[0], out_weight[0])
    local_mix = (tokens.astype(jnp.float32) + window_join(window_terms, CHANNELS)).astype(jnp.bfloat16)
    after_local = feed_forward(local_mix, norm_gains[1], up_weight[0], down_weight[0])
    grid_terms = attention_terms(grid_split(after_local, CHANNELS), norm_gains[2], qkv_weight[1], out_weight[1]).astype(jnp.bfloat16)
    global_mix = (after_local.astype(jnp.float32) + grid_join(grid_terms, CHANNELS).astype(jnp.float32)).astype(jnp.bfloat16)
    return feed_forward(global_mix, norm_gains[3], up_weight[1], down_weight[1])
```

```python
import math

import jax
import jax.numpy as jnp
from jax import lax
from jax.experimental import pallas as pl
from jax.experimental.pallas import tpu as pltpu
from jax.sharding import PartitionSpec as P

HEADS = 8
EPSILON = 1e-06
CHANNELS = 256
HEAD_DIM = CHANNELS // HEADS
SCORE_SCALE = math.log2(math.e) / math.sqrt(HEAD_DIM)
BANDS = 4
BAND_ROWS = 8
BREADTH = 128
BAND_TOKENS = BAND_ROWS * BREADTH
PEERS = 64
CHUNK = BAND_TOKENS // PEERS
BLOCK = 256
MESH = pl.DeviceIdType.MESH


def layer_norm(x, gain):
    centred = x - jnp.mean(x, axis=-1, keepdims=True)
    spread = jnp.mean(centred * centred, axis=-1, keepdims=True)
    return (centred * lax.rsqrt(spread + EPSILON) * gain).astype(jnp.bfloat16)


def dot(a, b):
    return jnp.dot(a, b, preferred_element_type=jnp.float32)


def feed_forward(mix, gain, up, down):
    normed = layer_norm(mix, gain)
    units = dot(normed, up)
    hidden = (0.5 * units) * (1.0 + lax.erf(units * math.sqrt(0.5)))
    return mix + dot(hidden.astype(jnp.bfloat16), down)


def spread_heads(x, masks):
    return jnp.concatenate(
        [x[16 * t : 16 * t + 16] * masks[h] for t in range(4) for h in range(HEADS)], axis=0
    )


def segment_max(x, lane):
    for d in (1, 2, 4, 8):
        partner = jnp.where((lane & d) == 0, pltpu.roll(x, 128 - d, 1), pltpu.roll(x, d, 1))
        x = jnp.maximum(x, partner)
    return x


def attend(qkv, masks, ones, lane):
    query = qkv[:, :CHANNELS]
    keys = spread_heads(qkv[:, CHANNELS : 2 * CHANNELS], masks)
    values = spread_heads(qkv[:, 2 * CHANNELS :], masks)
    scores = lax.dot_general(
        query, keys, (((1,), (1,)), ((), ())), preferred_element_type=jnp.float32
    )
    parts = [scores[:, 128 * t : 128 * t + 128] for t in range(4)]
    top = jnp.maximum(jnp.maximum(parts[0], parts[1]), jnp.maximum(parts[2], parts[3]))
    top = segment_max(top, lane)
    weights = jnp.concatenate(
        [jnp.exp2((p - top) * SCORE_SCALE).astype(jnp.bfloat16) for p in parts], axis=1
    )
    total = dot(weights, ones)
    return (dot(weights, values) / total).astype(jnp.bfloat16)


def attention(normed, qkv_weight, out_weight, masks, ones, lane):
    qkv = dot(normed, qkv_weight).astype(jnp.bfloat16)
    attended = [
        attend(qkv[64 * w : 64 * w + 64], masks, ones, lane) for w in range(normed.shape[0] // 64)
    ]
    return dot(jnp.concatenate(attended, axis=0), out_weight)


def kernel(
    tokens, gains, qkv_weight, out_weight, up_weight, down_weight, out,
    sent, recv, terms, back, regroup, ungroup,
    sent_sem, recv_sem, terms_sem, back_sem,
):
    row, col = lax.axis_index("rows"), lax.axis_index("cols")
    core = lax.rem(row, 2)
    me = (row // 2) * 8 + col

    def peer(k):
        p = lax.rem(me + k, PEERS)
        return p, (2 * (p // 8) + core, lax.rem(p, 8))

    barrier = pltpu.get_barrier_semaphore()

    @pl.loop(1, PEERS)
    def _(k):
        pl.semaphore_signal(barrier, inc=1, device_id=peer(k)[1], device_id_type=MESH)

    pl.semaphore_wait(barrier, PEERS - 1)

    def chunk(ref, b, p):
        return ref.at[b, pl.ds(pl.multiple_of(p * CHUNK, CHUNK), CHUNK)]

    def exchange(src, dst, b, src_sem, dst_sem):
        @pl.loop(1, PEERS)
        def _(k):
            p, device = peer(k)
            pltpu.make_async_remote_copy(
                src_ref=chunk(src, b, p), dst_ref=chunk(dst, b, me),
                send_sem=src_sem.at[b], recv_sem=dst_sem.at[b],
                device_id=device, device_id_type=MESH,
            ).start()

        pltpu.make_async_copy(chunk(src, b, me), chunk(dst, b, me), dst_sem.at[b]).start()

    def arrived(dst, b, dst_sem):
        pltpu.make_async_copy(dst.at[b], dst.at[b], dst_sem.at[b]).wait()

    def departed(src, b, src_sem):
        part = src.at[b, pl.ds(0, (PEERS - 1) * CHUNK)]
        pltpu.make_async_copy(part, part, src_sem.at[b]).wait()

    channel = lax.broadcasted_iota(jnp.int32, (1, CHANNELS), 1)
    masks = [(channel // HEAD_DIM == h).astype(jnp.bfloat16) for h in range(HEADS)]
    key_head = lax.broadcasted_iota(jnp.int32, (512, CHANNELS), 0) // 16 % HEADS
    channel_head = lax.broadcasted_iota(jnp.int32, (512, CHANNELS), 1) // HEAD_DIM
    ones = (key_head == channel_head).astype(jnp.bfloat16)
    lane = lax.broadcasted_iota(jnp.int32, (64, 128), 1)

    def window_block(b, j):
        x = []
        for p in range(2):
            strips = [
                tokens[b * 8 + r, pl.ds(pl.multiple_of(32 * j + 16 * p, 16), 16), :].astype(jnp.float32)
                for r in range(8)
            ]
            x += [s[:8] for s in strips] + [s[8:] for s in strips]
        x = jnp.concatenate(x, axis=0)
        normed = layer_norm(x, gains[0:1])
        mixed = x + attention(normed, qkv_weight[0], out_weight[0], masks, ones, lane)
        mixed = mixed.astype(jnp.bfloat16).astype(jnp.float32)
        y = feed_forward(mixed, gains[1:2], up_weight[0], down_weight[0])
        for p in range(2):
            for r in range(8):
                lo, hi = 128 * p + 8 * r, 128 * p + 64 + 8 * r
                strip = jnp.concatenate([y[lo : lo + 8], y[hi : hi + 8]], axis=0)
                place = pl.ds(pl.multiple_of(128 * r + 32 * j + 16 * p, 16), 16)
                sent[b, place, :] = strip.astype(jnp.bfloat16)

    def grid_block(b, j):
        x = jnp.concatenate(
            [
                jnp.concatenate(
                    [regroup[h, pl.ds(4 * j + i, 64, stride=CHUNK), :] for h in range(2)], axis=1
                )
                for i in range(4)
            ],
            axis=0,
        )
        normed = layer_norm(x, gains[2:3])
        y = attention(normed, qkv_weight[1], out_weight[1], masks, ones, lane)
        for i in range(4):
            for h in range(2):
                ungroup[h, pl.ds(4 * j + i, 64, stride=CHUNK), :] = y[
                    64 * i : 64 * i + 64, 128 * h : 128 * h + 128
                ]

    def final_block(b, j):
        place = pl.ds(pl.multiple_of(BLOCK * j, BLOCK), BLOCK)
        mixed = sent[b, place, :].astype(jnp.float32) + back[b, place, :].astype(jnp.float32)
        mixed = mixed.astype(jnp.bfloat16).astype(jnp.float32)
        y = feed_forward(mixed, gains[3:4], up_weight[1], down_weight[1])
        out[pl.ds(b * 8 + 2 * j, 2), :, :] = y.astype(jnp.bfloat16).reshape(2, BREADTH, CHANNELS)

    blocks = BAND_TOKENS // BLOCK

    @pl.loop(0, BANDS + 4)
    def _(t):
        @pl.when(t < BANDS)
        def _():
            @pl.loop(0, blocks)
            def _(j):
                window_block(t, j)

            exchange(sent, recv, t, sent_sem, recv_sem)

        @pl.when((t >= 2) & (t < BANDS + 2))
        def _():
            b = t - 2
            arrived(recv, b, recv_sem)
            @pl.loop(0, blocks)
            def _(j):
                place = pl.ds(pl.multiple_of(BLOCK * j, BLOCK), BLOCK)
                for h in range(2):
                    regroup[h, place, :] = recv[b, place, 128 * h : 128 * h + 128].astype(jnp.float32)

            @pl.loop(0, blocks)
            def _(j):
                grid_block(b, j)

            @pl.loop(0, blocks)
            def _(j):
                place = pl.ds(pl.multiple_of(BLOCK * j, BLOCK), BLOCK)
                for h in range(2):
                    terms[b, place, 128 * h : 128 * h + 128] = ungroup[h, place, :].astype(jnp.bfloat16)

            exchange(terms, back, b, terms_sem, back_sem)

        @pl.when(t >= 4)
        def _():
            b = t - 4
            arrived(back, b, back_sem)
            @pl.loop(0, blocks)
            def _(j):
                final_block(b, j)

    @pl.loop(0, BANDS)
    def _(b):
        departed(sent, b, sent_sem)
        departed(terms, b, terms_sem)


def on_device(tokens, norm_gains, qkv_weight, out_weight, up_weight, down_weight):
    band = pltpu.VMEM((BANDS, BAND_TOKENS, CHANNELS), jnp.bfloat16)
    halves = pltpu.VMEM((2, BAND_TOKENS, 128), jnp.float32)
    return pl.pallas_call(
        kernel,
        out_shape=jax.ShapeDtypeStruct(tokens.shape, jnp.bfloat16),
        in_specs=[pl.BlockSpec(memory_space=pltpu.VMEM)] * 6,
        out_specs=pl.BlockSpec(memory_space=pltpu.VMEM),
        scratch_shapes=[band] * 4 + [halves] * 2 + [pltpu.SemaphoreType.DMA((BANDS,))] * 4,
        compiler_params=pltpu.CompilerParams(
            collective_id=0, has_side_effects=True, vmem_limit_bytes=56 * 2**20
        ),
    )(tokens, norm_gains, qkv_weight, out_weight, up_weight, down_weight)


def solution(mesh):
    return jax.shard_map(
        on_device,
        mesh=mesh,
        in_specs=(P("rows", "cols", None), P(), P(), P(), P(), P()),
        out_specs=P("rows", "cols", None),
        check_vma=False,
    )
```

```python
import math

import jax
import jax.numpy as jnp
from jax import lax
from jax.experimental import pallas as pl
from jax.experimental.pallas import tpu as pltpu
from jax.sharding import PartitionSpec as P

HEADS = 8
EPSILON = 1e-06
CHANNELS = 256
HEAD_DIM = CHANNELS // HEADS
SCORE_SCALE = math.log2(math.e) / math.sqrt(HEAD_DIM)
BANDS = 4
BAND_ROWS = 8
BREADTH = 128
BAND_TOKENS = BAND_ROWS * BREADTH
PEERS = 64
CHUNK = BAND_TOKENS // PEERS
BLOCK = 256
FINAL = 1024
PAIRS = 8
GROUPS = 16
MESH = pl.DeviceIdType.MESH


def layer_norm(x, gain):
    centred = x - jnp.mean(x, axis=-1, keepdims=True)
    spread = jnp.mean(centred * centred, axis=-1, keepdims=True)
    return (centred * lax.rsqrt(spread + EPSILON) * gain).astype(jnp.bfloat16)


def dot(a, b):
    return jnp.dot(a, b, preferred_element_type=jnp.float32)


def feed_forward(mix, gain, up, down):
    normed = layer_norm(mix, gain)
    units = dot(normed, up)
    hidden = (0.5 * units) * (1.0 + lax.erf(units * math.sqrt(0.5)))
    return mix + dot(hidden.astype(jnp.bfloat16), down)


def spread_heads(x, masks):
    return jnp.concatenate(
        [x[16 * t : 16 * t + 16] * masks[h] for t in range(4) for h in range(HEADS)], axis=0
    )


def segment_max(x, lane):
    for d in (1, 2, 4, 8):
        partner = jnp.where((lane & d) == 0, pltpu.roll(x, 128 - d, 1), pltpu.roll(x, d, 1))
        x = jnp.maximum(x, partner)
    return x


def attention(normed, qkv_weight, out_weight, masks, ones, lane):
    qkv = dot(normed, qkv_weight).astype(jnp.bfloat16)
    groups = [slice(64 * w, 64 * w + 64) for w in range(normed.shape[0] // 64)]
    keys = [spread_heads(qkv[g, CHANNELS : 2 * CHANNELS], masks) for g in groups]
    scores = [
        lax.dot_general(
            qkv[g, :CHANNELS], k, (((1,), (1,)), ((), ())), preferred_element_type=jnp.float32
        )
        for g, k in zip(groups, keys)
    ]
    scores = jnp.concatenate(scores, axis=0)
    parts = [scores[:, 128 * t : 128 * t + 128] for t in range(4)]
    top = jnp.maximum(jnp.maximum(parts[0], parts[1]), jnp.maximum(parts[2], parts[3]))
    top = segment_max(top, lane)
    weights = jnp.concatenate(
        [jnp.exp2((p - top) * SCORE_SCALE).astype(jnp.bfloat16) for p in parts], axis=1
    )
    total = dot(weights, ones)
    values = [spread_heads(qkv[g, 2 * CHANNELS :], masks) for g in groups]
    mixed = jnp.concatenate([dot(weights[g], v) for g, v in zip(groups, values)], axis=0)
    return dot((mixed / total).astype(jnp.bfloat16), out_weight)


def kernel(
    tokens, gains, qkv_weight, out_weight, up_weight, down_weight, out,
    sent, recv, terms, back, regroup, ungroup,
    sent_sem, recv_sem, terms_sem, back_sem,
):
    row, col = lax.axis_index("rows"), lax.axis_index("cols")
    core = lax.rem(row, 2)
    me = (row // 2) * 8 + col

    def peer(k):
        p = lax.rem(me + k, PEERS)
        return p, (2 * (p // 8) + core, lax.rem(p, 8))

    barrier = pltpu.get_barrier_semaphore()

    @pl.loop(1, PEERS)
    def _(k):
        pl.semaphore_signal(barrier, inc=1, device_id=peer(k)[1], device_id_type=MESH)

    pl.semaphore_wait(barrier, PEERS - 1)

    def chunk(ref, b, p):
        return ref.at[b, pl.ds(pl.multiple_of(p * CHUNK, CHUNK), CHUNK)]

    def exchange(src, dst, b, src_sem, dst_sem):
        @pl.loop(1, PEERS)
        def _(k):
            p, device = peer(k)
            pltpu.make_async_remote_copy(
                src_ref=chunk(src, b, p), dst_ref=chunk(dst, b, me),
                send_sem=src_sem.at[b], recv_sem=dst_sem.at[b],
                device_id=device, device_id_type=MESH,
            ).start()

        pltpu.make_async_copy(chunk(src, b, me), chunk(dst, b, me), dst_sem.at[b]).start()

    def arrived(dst, b, dst_sem):
        pltpu.make_async_copy(dst.at[b], dst.at[b], dst_sem.at[b]).wait()

    def departed(src, b, src_sem):
        part = src.at[b, pl.ds(0, (PEERS - 1) * CHUNK)]
        pltpu.make_async_copy(part, part, src_sem.at[b]).wait()

    channel = lax.broadcasted_iota(jnp.int32, (1, CHANNELS), 1)
    masks = [(channel // HEAD_DIM == h).astype(jnp.bfloat16) for h in range(HEADS)]
    key_head = lax.broadcasted_iota(jnp.int32, (512, CHANNELS), 0) // 16 % HEADS
    channel_head = lax.broadcasted_iota(jnp.int32, (512, CHANNELS), 1) // HEAD_DIM
    ones = (key_head == channel_head).astype(jnp.bfloat16)
    lane = lax.broadcasted_iota(jnp.int32, (1, 128), 1)

    def window_block(b, j):
        x = []
        for p in range(PAIRS):
            strips = [
                tokens[b * 8 + r, pl.ds(pl.multiple_of(16 * (PAIRS * j + p), 16), 16), :].astype(jnp.float32)
                for r in range(8)
            ]
            x += [s[:8] for s in strips] + [s[8:] for s in strips]
        x = jnp.concatenate(x, axis=0)
        normed = layer_norm(x, gains[0:1])
        mixed = x + attention(normed, qkv_weight[0], out_weight[0], masks, ones, lane)
        mixed = mixed.astype(jnp.bfloat16).astype(jnp.float32)
        y = feed_forward(mixed, gains[1:2], up_weight[0], down_weight[0])
        for p in range(PAIRS):
            for r in range(8):
                lo, hi = 128 * p + 8 * r, 128 * p + 64 + 8 * r
                strip = jnp.concatenate([y[lo : lo + 8], y[hi : hi + 8]], axis=0)
                place = pl.ds(pl.multiple_of(128 * r + 16 * (PAIRS * j + p), 16), 16)
                sent[b, place, :] = strip.astype(jnp.bfloat16)

    def grid_block(b, j):
        x = jnp.concatenate(
            [
                jnp.concatenate(
                    [regroup[h, pl.ds(GROUPS * j + i, 64, stride=CHUNK), :] for h in range(2)], axis=1
                )
                for i in range(GROUPS)
            ],
            axis=0,
        )
        normed = layer_norm(x, gains[2:3])
        y = attention(normed, qkv_weight[1], out_weight[1], masks, ones, lane)
        for i in range(GROUPS):
            for h in range(2):
                ungroup[h, pl.ds(GROUPS * j + i, 64, stride=CHUNK), :] = y[
                    64 * i : 64 * i + 64, 128 * h : 128 * h + 128
                ]

    def final_block(b, j):
        place = pl.ds(pl.multiple_of(FINAL * j, FINAL), FINAL)
        mixed = sent[b, place, :].astype(jnp.float32) + back[b, place, :].astype(jnp.float32)
        mixed = mixed.astype(jnp.bfloat16).astype(jnp.float32)
        y = feed_forward(mixed, gains[3:4], up_weight[1], down_weight[1])
        out[pl.ds(b * 8 + FINAL // BREADTH * j, FINAL // BREADTH), :, :] = y.astype(jnp.bfloat16).reshape(FINAL // BREADTH, BREADTH, CHANNELS)

    blocks = BAND_TOKENS // BLOCK

    @pl.loop(0, BANDS + 4)
    def _(t):
        @pl.when(t < BANDS)
        def _():
            @pl.loop(0, 8 // PAIRS)
            def _(j):
                window_block(t, j)

            exchange(sent, recv, t, sent_sem, recv_sem)

        @pl.when((t >= 2) & (t < BANDS + 2))
        def _():
            b = t - 2
            arrived(recv, b, recv_sem)
            @pl.loop(0, blocks)
            def _(j):
                place = pl.ds(pl.multiple_of(BLOCK * j, BLOCK), BLOCK)
                for h in range(2):
                    regroup[h, place, :] = recv[b, place, 128 * h : 128 * h + 128].astype(jnp.float32)

            @pl.loop(0, 16 // GROUPS)
            def _(j):
                grid_block(b, j)

            @pl.loop(0, blocks)
            def _(j):
                place = pl.ds(pl.multiple_of(BLOCK * j, BLOCK), BLOCK)
                for h in range(2):
                    terms[b, place, 128 * h : 128 * h + 128] = ungroup[h, place, :].astype(jnp.bfloat16)

            exchange(terms, back, b, terms_sem, back_sem)

        @pl.when(t >= 4)
        def _():
            b = t - 4
            arrived(back, b, back_sem)
            @pl.loop(0, BAND_TOKENS // FINAL)
            def _(j):
                final_block(b, j)

    @pl.loop(0, BANDS)
    def _(b):
        departed(sent, b, sent_sem)
        departed(terms, b, terms_sem)


def on_device(tokens, norm_gains, qkv_weight, out_weight, up_weight, down_weight):
    band = pltpu.VMEM((BANDS, BAND_TOKENS, CHANNELS), jnp.bfloat16)
    halves = pltpu.VMEM((2, BAND_TOKENS, 128), jnp.float32)
    return pl.pallas_call(
        kernel,
        out_shape=jax.ShapeDtypeStruct(tokens.shape, jnp.bfloat16),
        in_specs=[pl.BlockSpec(memory_space=pltpu.VMEM)] * 6,
        out_specs=pl.BlockSpec(memory_space=pltpu.VMEM),
        scratch_shapes=[band] * 4 + [halves] * 2 + [pltpu.SemaphoreType.DMA((BANDS,))] * 4,
        compiler_params=pltpu.CompilerParams(
            collective_id=0, has_side_effects=True, vmem_limit_bytes=56 * 2**20
        ),
    )(tokens, norm_gains, qkv_weight, out_weight, up_weight, down_weight)


def solution(mesh):
    return jax.shard_map(
        on_device,
        mesh=mesh,
        in_specs=(P("rows", "cols", None), P(), P(), P(), P(), P()),
        out_specs=P("rows", "cols", None),
        check_vma=False,
    )
```

```python
import math

import jax
import jax.numpy as jnp
from jax import lax
from jax.experimental import pallas as pl
from jax.experimental.pallas import tpu as pltpu
from jax.sharding import PartitionSpec as P

HEADS = 8
EPSILON = 1e-06
CHANNELS = 256
HEAD_DIM = CHANNELS // HEADS
SCORE_SCALE = math.log2(math.e) / math.sqrt(HEAD_DIM)
BANDS = 4
BAND_ROWS = 8
BREADTH = 128
BAND_TOKENS = BAND_ROWS * BREADTH
PEERS = 64
CHUNK = BAND_TOKENS // PEERS
WINDOW_STRAND = 512
GRID_STRAND = 512
FINAL_STRAND = 256
MESH = pl.DeviceIdType.MESH


def layer_norm(x, gain):
    centred = x - jnp.mean(x, axis=-1, keepdims=True)
    spread = jnp.mean(centred * centred, axis=-1, keepdims=True)
    return (centred * lax.rsqrt(spread + EPSILON) * gain).astype(jnp.bfloat16)


def dot(a, b):
    return jnp.dot(a, b, preferred_element_type=jnp.float32)


def interleave(strands):
    waiting, active = list(strands), []
    while waiting or active:
        if waiting:
            active.append(waiting.pop(0))
        for strand in list(active):
            if next(strand, strand) is strand:
                active.remove(strand)


def feed_forward(mix, gain, up, down):
    normed = layer_norm(mix, gain)
    yield
    twice = []
    for c in range(0, up.shape[1], 512):
        units = dot(normed, up[:, c : c + 512])
        twice.append((units + units * lax.erf(units * math.sqrt(0.5))).astype(jnp.bfloat16))
        yield
    return mix + 0.5 * dot(jnp.concatenate(twice, axis=1), down[...])


def spread_heads(x, masks):
    zero = jnp.zeros((16, 128), x.dtype)
    rows = []
    for t in range(4):
        low, high = x[16 * t : 16 * t + 16, :128], x[16 * t : 16 * t + 16, 128:]
        rows += [jnp.concatenate([low * m, zero], axis=1) for m in masks]
        rows += [jnp.concatenate([zero, high * m], axis=1) for m in masks]
    return jnp.concatenate(rows, axis=0)


def segment_max(x, lane, d=8):
    if d == 0:
        return x
    half = x.shape[0] // 2
    a, b = x[:half], x[half:]
    first = (lane & d) == 0
    both = jnp.where(
        first,
        jnp.maximum(a, pltpu.roll(a, 128 - d, 1)),
        jnp.maximum(b, pltpu.roll(b, d, 1)),
    )
    both = segment_max(both, lane, d // 2)
    return jnp.concatenate(
        [jnp.where(first, both, pltpu.roll(both, d, 1)), jnp.where(first, pltpu.roll(both, 128 - d, 1), both)],
        axis=0,
    )


def attention(normed, qkv_weight, out_weight, masks, ones, lane):
    qkv = dot(normed, qkv_weight[...]).astype(jnp.bfloat16)
    yield
    groups = [slice(64 * w, 64 * w + 64) for w in range(normed.shape[0] // 64)]
    scores = [
        lax.dot_general(
            qkv[g, :CHANNELS],
            spread_heads(qkv[g, CHANNELS : 2 * CHANNELS], masks),
            (((1,), (1,)), ((), ())),
            preferred_element_type=jnp.float32,
        )
        for g in groups
    ]
    scores = jnp.concatenate(scores, axis=0)
    parts = [scores[:, 128 * t : 128 * t + 128] for t in range(4)]
    top = jnp.maximum(jnp.maximum(parts[0], parts[1]), jnp.maximum(parts[2], parts[3]))
    yield
    top = segment_max(top, lane)
    yield
    weights = [jnp.exp2((p - top) * SCORE_SCALE) for p in parts]
    total = (weights[0] + weights[1]) + (weights[2] + weights[3])
    coarse = total.astype(jnp.bfloat16)
    fine = (total - coarse.astype(jnp.float32)).astype(jnp.bfloat16)
    total = dot(jnp.concatenate([coarse, fine], axis=1), ones)
    weights = jnp.concatenate([w.astype(jnp.bfloat16) for w in weights], axis=1)
    yield
    mixed = [
        dot(weights[g], spread_heads(qkv[g, 2 * CHANNELS :], masks)) for g in groups
    ]
    mixed = (jnp.concatenate(mixed, axis=0) / total).astype(jnp.bfloat16)
    yield
    return dot(mixed, out_weight[...])


def kernel(
    tokens_hbm, gains_hbm, qkv_hbm, out_hbm, up_hbm, down_hbm, result_hbm,
    tokens, gains, qkv_weight, out_weight, up_weight, down_weight, result,
    sent, recv, terms, back, regroup, ungroup,
    token_sem, gain_sem, weight_sem, result_sem, sent_sem, recv_sem, terms_sem, back_sem,
):
    row, col = lax.axis_index("rows"), lax.axis_index("cols")
    core, place_row = lax.rem(row, 2), lax.div(row, 2)
    me = place_row * 8 + col

    def load_tokens(b):
        rows = pl.ds(b * BAND_ROWS, BAND_ROWS)
        return pltpu.make_async_copy(tokens_hbm.at[rows], tokens.at[rows], token_sem.at[b])

    def load_weights(i):
        pairs = ((qkv_hbm, qkv_weight), (out_hbm, out_weight), (up_hbm, up_weight), (down_hbm, down_weight))
        return [
            pltpu.make_async_copy(src.at[i], dst.at[i], weight_sem.at[i, n])
            for n, (src, dst) in enumerate(pairs)
        ]

    def store_result(b):
        rows = pl.ds(b * BAND_ROWS, BAND_ROWS)
        return pltpu.make_async_copy(result.at[rows], result_hbm.at[rows], result_sem.at[b])

    load_gains = pltpu.make_async_copy(gains_hbm, gains, gain_sem)
    load_gains.start()
    load_tokens(0).start()
    for copy in load_weights(0):
        copy.start()
    for b in range(1, BANDS):
        load_tokens(b).start()
    for copy in load_weights(1):
        copy.start()

    peer_cols = [lax.rem(col + c, 8) for c in range(8)]

    def each_peer(act):
        @pl.loop(0, 8)
        def _(a):
            r = lax.rem(place_row + a, 8)
            for c in range(1, 8):
                act(r * 8 + peer_cols[c], (2 * r + core, peer_cols[c]))

        @pl.loop(1, 8)
        def _(a):
            r = lax.rem(place_row + a, 8)
            act(r * 8 + col, (2 * r + core, col))

    barrier = pltpu.get_barrier_semaphore()
    each_peer(
        lambda p, device: pl.semaphore_signal(barrier, inc=1, device_id=device, device_id_type=MESH)
    )

    def chunk(ref, b, p):
        return ref.at[b, pl.ds(pl.multiple_of(p * CHUNK, CHUNK), CHUNK)]

    def exchange(src, dst, b, src_sem, dst_sem):
        each_peer(
            lambda p, device: pltpu.make_async_remote_copy(
                src_ref=chunk(src, b, p), dst_ref=chunk(dst, b, me),
                send_sem=src_sem.at[b], recv_sem=dst_sem.at[b],
                device_id=device, device_id_type=MESH,
            ).start()
        )
        pltpu.make_async_copy(chunk(src, b, me), chunk(dst, b, me), dst_sem.at[b]).start()

    def arrived(dst, b, dst_sem):
        pltpu.make_async_copy(dst.at[b], dst.at[b], dst_sem.at[b]).wait()

    def departed(src, b, src_sem):
        part = src.at[b, pl.ds(0, (PEERS - 1) * CHUNK)]
        pltpu.make_async_copy(part, part, src_sem.at[b]).wait()

    channel = lax.broadcasted_iota(jnp.int32, (1, 128), 1)
    masks = [(channel // HEAD_DIM == j).astype(jnp.bfloat16) for j in range(4)]
    key_head = lax.broadcasted_iota(jnp.int32, (CHANNELS, CHANNELS), 0) // 16 % HEADS
    channel_head = lax.broadcasted_iota(jnp.int32, (CHANNELS, CHANNELS), 1) // HEAD_DIM
    ones = (key_head == channel_head).astype(jnp.bfloat16)
    lane = lax.broadcasted_iota(jnp.int32, (1, 128), 1)

    def window_strand(b, first):
        pairs = range(first // 128, (first + WINDOW_STRAND) // 128)
        x = []
        for p in pairs:
            strips = [
                tokens[b * BAND_ROWS + r, 16 * p : 16 * p + 16, :].astype(jnp.float32) for r in range(8)
            ]
            x += [s[:8] for s in strips] + [s[8:] for s in strips]
        x = jnp.concatenate(x, axis=0)
        normed = layer_norm(x, gains[0:1])
        yield
        terms_a = yield from attention(normed, qkv_weight.at[0], out_weight.at[0], masks, ones, lane)
        mixed = (x + terms_a).astype(jnp.bfloat16).astype(jnp.float32)
        yield
        y = yield from feed_forward(mixed, gains[1:2], up_weight.at[0], down_weight.at[0])
        for n, p in enumerate(pairs):
            for r in range(8):
                lo, hi = 128 * n + 8 * r, 128 * n + 64 + 8 * r
                strip = jnp.concatenate([y[lo : lo + 8], y[hi : hi + 8]], axis=0)
                sent[b, 128 * r + 16 * p : 128 * r + 16 * p + 16, :] = strip.astype(jnp.bfloat16)

    def grid_strand(first):
        members = range(first // 64, (first + GRID_STRAND) // 64)
        x = jnp.concatenate(
            [
                jnp.concatenate([regroup[h, pl.ds(g, 64, stride=CHUNK), :] for h in range(2)], axis=1)
                for g in members
            ],
            axis=0,
        )
        normed = layer_norm(x, gains[2:3])
        yield
        y = yield from attention(normed, qkv_weight.at[1], out_weight.at[1], masks, ones, lane)
        for n, g in enumerate(members):
            for h in range(2):
                ungroup[h, pl.ds(g, 64, stride=CHUNK), :] = y[
                    64 * n : 64 * n + 64, 128 * h : 128 * h + 128
                ]

    def final_strand(b, first):
        span = pl.ds(first, FINAL_STRAND)
        mixed = sent[b, span, :].astype(jnp.float32) + back[b, span, :].astype(jnp.float32)
        mixed = mixed.astype(jnp.bfloat16).astype(jnp.float32)
        yield
        y = yield from feed_forward(mixed, gains[3:4], up_weight.at[1], down_weight.at[1])
        rows = FINAL_STRAND // BREADTH
        result[pl.ds(b * BAND_ROWS + first // BREADTH, rows), :, :] = y.astype(jnp.bfloat16).reshape(
            rows, BREADTH, CHANNELS
        )

    @pl.loop(0, BANDS + 4)
    def _(t):
        @pl.when(t == 0)
        def _():
            load_gains.wait()
            for copy in load_weights(0):
                copy.wait()

        @pl.when(t < BANDS)
        def _():
            load_tokens(t).wait()
            interleave(window_strand(t, f) for f in range(0, BAND_TOKENS, WINDOW_STRAND))

        @pl.when(t == 0)
        def _():
            pl.semaphore_wait(barrier, PEERS - 1)
            for copy in load_weights(1):
                copy.wait()

        @pl.when(t < BANDS)
        def _():
            exchange(sent, recv, t, sent_sem, recv_sem)

        @pl.when((t >= 2) & (t < BANDS + 2))
        def _():
            b = t - 2
            arrived(recv, b, recv_sem)
            for h in range(2):
                regroup[h] = recv[b, :, 128 * h : 128 * h + 128].astype(jnp.float32)
            interleave(grid_strand(f) for f in range(0, BAND_TOKENS, GRID_STRAND))
            for h in range(2):
                terms[b, :, 128 * h : 128 * h + 128] = ungroup[h].astype(jnp.bfloat16)
            exchange(terms, back, b, terms_sem, back_sem)

        @pl.when(t >= 4)
        def _():
            b = t - 4
            arrived(back, b, back_sem)
            interleave(final_strand(b, f) for f in range(0, BAND_TOKENS, FINAL_STRAND))
            store_result(b).start()

    @pl.loop(0, BANDS)
    def _(b):
        departed(sent, b, sent_sem)
        departed(terms, b, terms_sem)
        store_result(b).wait()


def on_device(tokens, norm_gains, qkv_weight, out_weight, up_weight, down_weight):
    arrays = (tokens, norm_gains, qkv_weight, out_weight, up_weight, down_weight)
    band = pltpu.VMEM((BANDS, BAND_TOKENS, CHANNELS), jnp.bfloat16)
    halves = pltpu.VMEM((2, BAND_TOKENS, 128), jnp.float32)
    return pl.pallas_call(
        kernel,
        out_shape=jax.ShapeDtypeStruct(tokens.shape, jnp.bfloat16),
        in_specs=[pl.BlockSpec(memory_space=pl.ANY)] * 6,
        out_specs=pl.BlockSpec(memory_space=pl.ANY),
        scratch_shapes=[pltpu.VMEM(a.shape, a.dtype) for a in arrays]
        + [pltpu.VMEM(tokens.shape, jnp.bfloat16)]
        + [band] * 4
        + [halves] * 2
        + [
            pltpu.SemaphoreType.DMA((BANDS,)),
            pltpu.SemaphoreType.DMA,
            pltpu.SemaphoreType.DMA((2, 4)),
        ]
        + [pltpu.SemaphoreType.DMA((BANDS,))] * 5,
        compiler_params=pltpu.CompilerParams(
            collective_id=0, has_side_effects=True, vmem_limit_bytes=56 * 2**20
        ),
    )(*arrays)


def solution(mesh):
    return jax.shard_map(
        on_device,
        mesh=mesh,
        in_specs=(P("rows", "cols", None), P(), P(), P(), P(), P()),
        out_specs=P("rows", "cols", None),
        check_vma=False,
    )
```

```python
import math

import jax
import jax.numpy as jnp
from jax import lax
from jax.experimental import pallas as pl
from jax.experimental.pallas import tpu as pltpu
from jax.sharding import PartitionSpec as P

HEADS = 8
EPSILON = 1e-06
CHANNELS = 256
HEAD_DIM = CHANNELS // HEADS
SCORE_SCALE = math.log2(math.e) / math.sqrt(HEAD_DIM)
BANDS = 4
BAND_ROWS = 8
BREADTH = 128
BAND_TOKENS = BAND_ROWS * BREADTH
PEERS = 64
CHUNK = BAND_TOKENS // PEERS
WINDOW_STRAND = 512
GRID_STRAND = 512
FINAL_STRAND = 256
MESH = pl.DeviceIdType.MESH


def layer_norm(x, gain):
    centred = x - jnp.mean(x, axis=-1, keepdims=True)
    spread = jnp.mean(centred * centred, axis=-1, keepdims=True)
    return (centred * lax.rsqrt(spread + EPSILON) * gain).astype(jnp.bfloat16)


def dot(a, b):
    return jnp.dot(a, b, preferred_element_type=jnp.float32)


def interleave(strands):
    waiting, active = list(strands), []
    while waiting or active:
        if waiting:
            active.append(waiting.pop(0))
        for strand in list(active):
            if next(strand, strand) is strand:
                active.remove(strand)


def feed_forward(mix, gain, up, down):
    normed = layer_norm(mix, gain)
    yield
    twice = []
    for c in range(0, up.shape[1], 512):
        units = dot(normed, up[:, c : c + 512])
        twice.append((units + units * lax.erf(units * math.sqrt(0.5))).astype(jnp.bfloat16))
        yield
    return (mix + mix) + dot(jnp.concatenate(twice, axis=1), down[...])


def spread_heads(x, masks):
    zero = jnp.zeros((16, 128), x.dtype)
    rows = []
    for t in range(4):
        low, high = x[16 * t : 16 * t + 16, :128], x[16 * t : 16 * t + 16, 128:]
        rows += [jnp.concatenate([low * m, zero], axis=1) for m in masks]
        rows += [jnp.concatenate([zero, high * m], axis=1) for m in masks]
    return jnp.concatenate(rows, axis=0)


def segment_max(x, lane, d=8):
    if d == 0:
        return x
    half = x.shape[0] // 2
    a, b = x[:half], x[half:]
    first = (lane & d) == 0
    both = jnp.where(
        first,
        jnp.maximum(a, pltpu.roll(a, 128 - d, 1)),
        jnp.maximum(b, pltpu.roll(b, d, 1)),
    )
    both = segment_max(both, lane, d // 2)
    return jnp.concatenate(
        [jnp.where(first, both, pltpu.roll(both, d, 1)), jnp.where(first, pltpu.roll(both, 128 - d, 1), both)],
        axis=0,
    )


def attention(normed, qkv_weight, out_weight, masks, ones, lane):
    qkv = dot(normed, qkv_weight[...]).astype(jnp.bfloat16)
    yield
    groups = [slice(64 * w, 64 * w + 64) for w in range(normed.shape[0] // 64)]
    scores = [
        lax.dot_general(
            qkv[g, :CHANNELS],
            spread_heads(qkv[g, CHANNELS : 2 * CHANNELS], masks),
            (((1,), (1,)), ((), ())),
            preferred_element_type=jnp.float32,
        )
        for g in groups
    ]
    scores = jnp.concatenate(scores, axis=0)
    parts = [scores[:, 128 * t : 128 * t + 128] for t in range(4)]
    top = jnp.maximum(jnp.maximum(parts[0], parts[1]), jnp.maximum(parts[2], parts[3]))
    yield
    top = segment_max(top, lane)
    yield
    weights = [jnp.exp2((p - top) * SCORE_SCALE) for p in parts]
    total = (weights[0] + weights[1]) + (weights[2] + weights[3])
    coarse = total.astype(jnp.bfloat16)
    fine = (total - coarse.astype(jnp.float32)).astype(jnp.bfloat16)
    total = dot(jnp.concatenate([coarse, fine], axis=1), ones)
    weights = jnp.concatenate([w.astype(jnp.bfloat16) for w in weights], axis=1)
    yield
    mixed = [
        dot(weights[g], spread_heads(qkv[g, 2 * CHANNELS :], masks)) for g in groups
    ]
    mixed = (jnp.concatenate(mixed, axis=0) / total).astype(jnp.bfloat16)
    yield
    return dot(mixed, out_weight[...])


def kernel(
    tokens_hbm, gains_hbm, qkv_hbm, out_hbm, up_hbm, down_hbm, result,
    tokens, gains, qkv_weight, out_weight, up_weight, down_weight,
    sent, recv, terms, back, regroup, ungroup,
    token_sem, gain_sem, weight_sem, sent_sem, recv_sem, terms_sem, back_sem,
):
    row, col = lax.axis_index("rows"), lax.axis_index("cols")
    core, place_row = lax.rem(row, 2), lax.div(row, 2)
    me = place_row * 8 + col

    def load_tokens(b):
        rows = pl.ds(b * BAND_ROWS, BAND_ROWS)
        return pltpu.make_async_copy(tokens_hbm.at[rows], tokens.at[rows], token_sem.at[b])

    def load_weights(i):
        pairs = ((qkv_hbm, qkv_weight), (out_hbm, out_weight), (up_hbm, up_weight), (down_hbm, down_weight))
        return [
            pltpu.make_async_copy(src.at[i], dst.at[i], weight_sem.at[i, n])
            for n, (src, dst) in enumerate(pairs)
        ]

    load_gains = pltpu.make_async_copy(gains_hbm, gains, gain_sem)
    load_gains.start()
    load_tokens(0).start()
    for copy in load_weights(0):
        copy.start()
    for b in range(1, BANDS):
        load_tokens(b).start()
    for copy in load_weights(1):
        copy.start()

    peer_cols = [lax.rem(col + c, 8) for c in range(8)]

    def each_peer(act):
        @pl.loop(0, 8)
        def _(a):
            r = lax.rem(place_row + a, 8)
            for c in range(1, 8):
                act(r * 8 + peer_cols[c], (2 * r + core, peer_cols[c]))

        @pl.loop(1, 8)
        def _(a):
            r = lax.rem(place_row + a, 8)
            act(r * 8 + col, (2 * r + core, col))

    barrier = pltpu.get_barrier_semaphore()
    each_peer(
        lambda p, device: pl.semaphore_signal(barrier, inc=1, device_id=device, device_id_type=MESH)
    )

    def chunk(ref, b, p):
        return ref.at[b, pl.ds(pl.multiple_of(p * CHUNK, CHUNK), CHUNK)]

    def exchange(src, dst, b, src_sem, dst_sem):
        each_peer(
            lambda p, device: pltpu.make_async_remote_copy(
                src_ref=chunk(src, b, p), dst_ref=chunk(dst, b, me),
                send_sem=src_sem.at[b], recv_sem=dst_sem.at[b],
                device_id=device, device_id_type=MESH,
            ).start()
        )
        own = pl.ds(pl.multiple_of(me * CHUNK, CHUNK), CHUNK)
        dst[b, own, :] = src[b, own, :]

    def arrived(dst, b, dst_sem):
        part = dst.at[b, pl.ds(0, (PEERS - 1) * CHUNK)]
        pltpu.make_async_copy(part, part, dst_sem.at[b]).wait()

    def departed(src, b, src_sem):
        part = src.at[b, pl.ds(0, (PEERS - 1) * CHUNK)]
        pltpu.make_async_copy(part, part, src_sem.at[b]).wait()

    channel = lax.broadcasted_iota(jnp.int32, (1, 128), 1)
    masks = [(channel // HEAD_DIM == j).astype(jnp.bfloat16) for j in range(4)]
    key_head = lax.broadcasted_iota(jnp.int32, (CHANNELS, CHANNELS), 0) // 16 % HEADS
    channel_head = lax.broadcasted_iota(jnp.int32, (CHANNELS, CHANNELS), 1) // HEAD_DIM
    ones = (key_head == channel_head).astype(jnp.bfloat16)
    lane = lax.broadcasted_iota(jnp.int32, (1, 128), 1)

    def window_strand(b, first):
        pairs = range(first // 128, (first + WINDOW_STRAND) // 128)
        x = []
        for p in pairs:
            strips = [
                tokens[b * BAND_ROWS + r, 16 * p : 16 * p + 16, :].astype(jnp.float32) for r in range(8)
            ]
            x += [s[:8] for s in strips] + [s[8:] for s in strips]
        x = jnp.concatenate(x, axis=0)
        normed = layer_norm(x, gains[0:1])
        yield
        terms_a = yield from attention(normed, qkv_weight.at[0], out_weight.at[0], masks, ones, lane)
        mixed = (x + terms_a).astype(jnp.bfloat16).astype(jnp.float32)
        yield
        y = yield from feed_forward(mixed, gains[1:2], up_weight.at[0], down_weight.at[0])
        for n, p in enumerate(pairs):
            for r in range(8):
                lo, hi = 128 * n + 8 * r, 128 * n + 64 + 8 * r
                strip = 0.5 * jnp.concatenate([y[lo : lo + 8], y[hi : hi + 8]], axis=0)
                sent[b, 128 * r + 16 * p : 128 * r + 16 * p + 16, :] = strip.astype(jnp.bfloat16)

    def grid_strand(first):
        members = range(first // 64, (first + GRID_STRAND) // 64)
        x = jnp.concatenate(
            [
                jnp.concatenate([regroup[h, pl.ds(g, 64, stride=CHUNK), :] for h in range(2)], axis=1)
                for g in members
            ],
            axis=0,
        )
        normed = layer_norm(x, gains[2:3])
        yield
        y = yield from attention(normed, qkv_weight.at[1], out_weight.at[1], masks, ones, lane)
        for n, g in enumerate(members):
            for h in range(2):
                ungroup[h, pl.ds(g, 64, stride=CHUNK), :] = y[
                    64 * n : 64 * n + 64, 128 * h : 128 * h + 128
                ]

    def final_strand(b, first):
        span = pl.ds(first, FINAL_STRAND)
        mixed = sent[b, span, :].astype(jnp.float32) + back[b, span, :].astype(jnp.float32)
        mixed = mixed.astype(jnp.bfloat16).astype(jnp.float32)
        yield
        y = yield from feed_forward(mixed, gains[3:4], up_weight.at[1], down_weight.at[1])
        rows = FINAL_STRAND // BREADTH
        result[pl.ds(b * BAND_ROWS + first // BREADTH, rows), :, :] = y.astype(jnp.bfloat16).reshape(
            rows, BREADTH, CHANNELS
        )

    @pl.loop(0, BANDS + 4)
    def _(t):
        @pl.when(t == 0)
        def _():
            load_gains.wait()
            for copy in load_weights(0):
                copy.wait()

        @pl.when(t < BANDS)
        def _():
            load_tokens(t).wait()
            interleave(window_strand(t, f) for f in range(0, BAND_TOKENS, WINDOW_STRAND))

        @pl.when(t == 0)
        def _():
            pl.semaphore_wait(barrier, PEERS - 1)
            for copy in load_weights(1):
                copy.wait()

        @pl.when(t < BANDS)
        def _():
            exchange(sent, recv, t, sent_sem, recv_sem)

        @pl.when((t == 1) | ((t >= 3) & (t < BANDS + 2)))
        def _():
            b = jnp.where(t < 2, 0, t - 2)
            arrived(recv, b, recv_sem)
            for h in range(2):
                regroup[h] = recv[b, :, 128 * h : 128 * h + 128].astype(jnp.float32)
            interleave(grid_strand(f) for f in range(0, BAND_TOKENS, GRID_STRAND))
            for h in range(2):
                terms[b, :, 128 * h : 128 * h + 128] = ungroup[h].astype(jnp.bfloat16)
            exchange(terms, back, b, terms_sem, back_sem)

        @pl.when(t >= 4)
        def _():
            b = t - 4
            arrived(back, b, back_sem)
            interleave(final_strand(b, f) for f in range(0, BAND_TOKENS, FINAL_STRAND))

    @pl.loop(0, BANDS)
    def _(b):
        departed(sent, b, sent_sem)
        departed(terms, b, terms_sem)


def on_device(tokens, norm_gains, qkv_weight, out_weight, up_weight, down_weight):
    arrays = (tokens, norm_gains, qkv_weight, out_weight, up_weight, down_weight)
    band = pltpu.VMEM((BANDS, BAND_TOKENS, CHANNELS), jnp.bfloat16)
    halves = pltpu.VMEM((2, BAND_TOKENS, 128), jnp.float32)
    twice = pl.pallas_call(
        kernel,
        out_shape=pltpu.VMEM(tokens.shape, jnp.bfloat16),
        in_specs=[pl.BlockSpec(memory_space=pl.ANY)] * 6,
        out_specs=pl.BlockSpec(memory_space=pltpu.VMEM),
        scratch_shapes=[pltpu.VMEM(a.shape, a.dtype) for a in arrays]
        + [band] * 4
        + [halves] * 2
        + [
            pltpu.SemaphoreType.DMA((BANDS,)),
            pltpu.SemaphoreType.DMA,
            pltpu.SemaphoreType.DMA((2, 4)),
        ]
        + [pltpu.SemaphoreType.DMA((BANDS,))] * 4,
        compiler_params=pltpu.CompilerParams(
            collective_id=0, has_side_effects=True, vmem_limit_bytes=60 * 2**20
        ),
    )(*arrays)
    return twice * 0.5


def solution(mesh):
    return jax.shard_map(
        on_device,
        mesh=mesh,
        in_specs=(P("rows", "cols", None), P(), P(), P(), P(), P()),
        out_specs=P("rows", "cols", None),
        check_vma=False,
    )
```

```python
import math

import jax
import jax.numpy as jnp
from jax import lax
from jax.experimental import pallas as pl
from jax.experimental.pallas import tpu as pltpu
from jax.sharding import PartitionSpec as P

HEADS = 8
EPSILON = 1e-06
CHANNELS = 256
HEAD_DIM = CHANNELS // HEADS
SCORE_SCALE = math.log2(math.e) / math.sqrt(HEAD_DIM)
BANDS = 4
BAND_ROWS = 8
BREADTH = 128
BAND_TOKENS = BAND_ROWS * BREADTH
PEERS = 64
CHUNK = BAND_TOKENS // PEERS
WINDOW_STRAND = 512
GRID_STRAND = 512
FINAL_STRAND = 256
MESH = pl.DeviceIdType.MESH


def layer_norm(x, gain):
    centred = x - jnp.mean(x, axis=-1, keepdims=True)
    spread = jnp.mean(centred * centred, axis=-1, keepdims=True)
    return (centred * lax.rsqrt(spread + EPSILON) * gain).astype(jnp.bfloat16)


def dot(a, b):
    return jnp.dot(a, b, preferred_element_type=jnp.float32)


def interleave(strands):
    waiting, active = list(strands), []
    while waiting or active:
        if waiting:
            active.append(waiting.pop(0))
        for strand in list(active):
            if next(strand, strand) is strand:
                active.remove(strand)


def feed_forward(mix, gain, up, down):
    normed = layer_norm(mix, gain)
    yield
    twice = []
    for c in range(0, up.shape[1], 512):
        units = dot(normed, up[:, c : c + 512])
        twice.append((units + units * lax.erf(units * math.sqrt(0.5))).astype(jnp.bfloat16))
        yield
    return (mix + mix) + dot(jnp.concatenate(twice, axis=1), down[...])


def spread_heads(x, masks):
    zero = jnp.zeros((16, 128), x.dtype)
    rows = []
    for t in range(4):
        low, high = x[16 * t : 16 * t + 16, :128], x[16 * t : 16 * t + 16, 128:]
        rows += [jnp.concatenate([low * m, zero], axis=1) for m in masks]
        rows += [jnp.concatenate([zero, high * m], axis=1) for m in masks]
    return jnp.concatenate(rows, axis=0)


def segment_max(x, lane, d=8):
    if d == 0:
        return x
    half = x.shape[0] // 2
    a, b = x[:half], x[half:]
    first = (lane & d) == 0
    both = jnp.where(
        first,
        jnp.maximum(a, pltpu.roll(a, 128 - d, 1)),
        jnp.maximum(b, pltpu.roll(b, d, 1)),
    )
    both = segment_max(both, lane, d // 2)
    return jnp.concatenate(
        [jnp.where(first, both, pltpu.roll(both, d, 1)), jnp.where(first, pltpu.roll(both, 128 - d, 1), both)],
        axis=0,
    )


def attention(normed, qkv_weight, out_weight, masks, ones, lane):
    qkv = dot(normed, qkv_weight[...]).astype(jnp.bfloat16)
    yield
    groups = [slice(64 * w, 64 * w + 64) for w in range(normed.shape[0] // 64)]
    scores = [
        lax.dot_general(
            qkv[g, :CHANNELS],
            spread_heads(qkv[g, CHANNELS : 2 * CHANNELS], masks),
            (((1,), (1,)), ((), ())),
            preferred_element_type=jnp.float32,
        )
        for g in groups
    ]
    scores = jnp.concatenate(scores, axis=0)
    parts = [scores[:, 128 * t : 128 * t + 128] for t in range(4)]
    top = jnp.maximum(jnp.maximum(parts[0], parts[1]), jnp.maximum(parts[2], parts[3]))
    yield
    top = segment_max(top, lane)
    yield
    weights = [jnp.exp2((p - top) * SCORE_SCALE) for p in parts]
    total = (weights[0] + weights[1]) + (weights[2] + weights[3])
    coarse = total.astype(jnp.bfloat16)
    fine = (total - coarse.astype(jnp.float32)).astype(jnp.bfloat16)
    weights = jnp.concatenate([w.astype(jnp.bfloat16) for w in weights], axis=1)
    yield
    total = dot(jnp.concatenate([coarse, fine], axis=1), ones)
    mixed = [
        dot(weights[g], spread_heads(qkv[g, 2 * CHANNELS :], masks)) for g in groups
    ]
    mixed = (jnp.concatenate(mixed, axis=0) / total).astype(jnp.bfloat16)
    yield
    return dot(mixed, out_weight[...])


def kernel(
    tokens_hbm, gains_hbm, qkv_hbm, out_hbm, up_hbm, down_hbm, result,
    tokens, gains, qkv_weight, out_weight, up_weight, down_weight,
    sent, recv, terms, back, regroup, ungroup,
    token_sem, gain_sem, weight_sem, sent_sem, recv_sem, terms_sem, back_sem,
):
    row, col = lax.axis_index("rows"), lax.axis_index("cols")
    core, place_row = lax.rem(row, 2), lax.div(row, 2)
    me = place_row * 8 + col

    def load_tokens(b):
        rows = pl.ds(b * BAND_ROWS, BAND_ROWS)
        return pltpu.make_async_copy(tokens_hbm.at[rows], tokens.at[rows], token_sem.at[b])

    def load_weights(i):
        pairs = ((qkv_hbm, qkv_weight), (out_hbm, out_weight), (up_hbm, up_weight), (down_hbm, down_weight))
        return [
            pltpu.make_async_copy(src.at[i], dst.at[i], weight_sem.at[i, n])
            for n, (src, dst) in enumerate(pairs)
        ]

    load_gains = pltpu.make_async_copy(gains_hbm, gains, gain_sem)
    load_gains.start()
    load_tokens(0).start()
    for copy in load_weights(0):
        copy.start()
    peer_cols = [lax.rem(col + c, 8) for c in range(8)]

    def each_peer(act):
        for a in range(8):
            r = lax.rem(place_row + a, 8)
            for c in range(8):
                if a + c > 0:
                    act(r * 8 + peer_cols[c], (2 * r + core, peer_cols[c]))

    barrier = pltpu.get_barrier_semaphore()
    each_peer(
        lambda p, device: pl.semaphore_signal(barrier, inc=1, device_id=device, device_id_type=MESH)
    )

    def chunk(ref, b, p):
        return ref.at[b, pl.ds(pl.multiple_of(p * CHUNK, CHUNK), CHUNK)]

    def exchange(src, dst, b, src_sem, dst_sem):
        each_peer(
            lambda p, device: pltpu.make_async_remote_copy(
                src_ref=chunk(src, b, p), dst_ref=chunk(dst, b, me),
                send_sem=src_sem.at[b], recv_sem=dst_sem.at[b],
                device_id=device, device_id_type=MESH,
            ).start()
        )
        own = pl.ds(pl.multiple_of(me * CHUNK, CHUNK), CHUNK)
        dst[b, own, :] = src[b, own, :]

    def arrived(dst, b, dst_sem):
        part = dst.at[b, pl.ds(0, (PEERS - 1) * CHUNK)]
        pltpu.make_async_copy(part, part, dst_sem.at[b]).wait()

    def departed(src, b, src_sem):
        part = src.at[b, pl.ds(0, (PEERS - 1) * CHUNK)]
        pltpu.make_async_copy(part, part, src_sem.at[b]).wait()

    channel = lax.broadcasted_iota(jnp.int32, (1, 128), 1)
    masks = [(channel // HEAD_DIM == j).astype(jnp.bfloat16) for j in range(4)]
    key_head = lax.broadcasted_iota(jnp.int32, (CHANNELS, CHANNELS), 0) // 16 % HEADS
    channel_head = lax.broadcasted_iota(jnp.int32, (CHANNELS, CHANNELS), 1) // HEAD_DIM
    ones = (key_head == channel_head).astype(jnp.bfloat16)
    lane = lax.broadcasted_iota(jnp.int32, (1, 128), 1)

    def window_strand(b, first):
        pairs = range(first // 128, (first + WINDOW_STRAND) // 128)
        x = []
        for p in pairs:
            strips = [
                tokens[b * BAND_ROWS + r, 16 * p : 16 * p + 16, :].astype(jnp.float32) for r in range(8)
            ]
            x += [s[:8] for s in strips] + [s[8:] for s in strips]
        x = jnp.concatenate(x, axis=0)
        normed = layer_norm(x, gains[0:1])
        yield
        terms_a = yield from attention(normed, qkv_weight.at[0], out_weight.at[0], masks, ones, lane)
        mixed = (x + terms_a).astype(jnp.bfloat16).astype(jnp.float32)
        yield
        y = yield from feed_forward(mixed, gains[1:2], up_weight.at[0], down_weight.at[0])
        for n, p in enumerate(pairs):
            for r in range(8):
                lo, hi = 128 * n + 8 * r, 128 * n + 64 + 8 * r
                strip = 0.5 * jnp.concatenate([y[lo : lo + 8], y[hi : hi + 8]], axis=0)
                sent[b, 128 * r + 16 * p : 128 * r + 16 * p + 16, :] = strip.astype(jnp.bfloat16)

    def grid_strand(first):
        members = range(first // 64, (first + GRID_STRAND) // 64)
        x = jnp.concatenate(
            [
                jnp.concatenate([regroup[h, pl.ds(g, 64, stride=CHUNK), :] for h in range(2)], axis=1)
                for g in members
            ],
            axis=0,
        )
        normed = layer_norm(x, gains[2:3])
        yield
        y = yield from attention(normed, qkv_weight.at[1], out_weight.at[1], masks, ones, lane)
        for n, g in enumerate(members):
            for h in range(2):
                ungroup[h, pl.ds(g, 64, stride=CHUNK), :] = y[
                    64 * n : 64 * n + 64, 128 * h : 128 * h + 128
                ]

    def final_strand(b, first):
        span = pl.ds(first, FINAL_STRAND)
        mixed = sent[b, span, :].astype(jnp.float32) + back[b, span, :].astype(jnp.float32)
        mixed = mixed.astype(jnp.bfloat16).astype(jnp.float32)
        yield
        y = yield from feed_forward(mixed, gains[3:4], up_weight.at[1], down_weight.at[1])
        rows = FINAL_STRAND // BREADTH
        result[pl.ds(b * BAND_ROWS + first // BREADTH, rows), :, :] = y.astype(jnp.bfloat16).reshape(
            rows, BREADTH, CHANNELS
        )

    @pl.loop(0, BANDS + 4)
    def _(t):
        @pl.when(t == 0)
        def _():
            load_gains.wait()
            for copy in load_weights(0):
                copy.wait()
            for b in range(1, BANDS):
                load_tokens(b).start()
            for copy in load_weights(1):
                copy.start()

        @pl.when(t < BANDS)
        def _():
            load_tokens(t).wait()
            interleave(window_strand(t, f) for f in range(0, BAND_TOKENS, WINDOW_STRAND))

        @pl.when(t == 0)
        def _():
            pl.semaphore_wait(barrier, PEERS - 1)
            for copy in load_weights(1):
                copy.wait()

        @pl.when(t < BANDS)
        def _():
            exchange(sent, recv, t, sent_sem, recv_sem)

        @pl.when((t == 1) | ((t >= 3) & (t < BANDS + 2)))
        def _():
            b = jnp.where(t < 2, 0, t - 2)
            arrived(recv, b, recv_sem)
            for h in range(2):
                regroup[h] = recv[b, :, 128 * h : 128 * h + 128].astype(jnp.float32)
            interleave(grid_strand(f) for f in range(0, BAND_TOKENS, GRID_STRAND))
            for h in range(2):
                terms[b, :, 128 * h : 128 * h + 128] = ungroup[h].astype(jnp.bfloat16)
            exchange(terms, back, b, terms_sem, back_sem)

        @pl.when(t >= 4)
        def _():
            b = t - 4
            arrived(back, b, back_sem)
            interleave(final_strand(b, f) for f in range(0, BAND_TOKENS, FINAL_STRAND))

    @pl.loop(0, BANDS)
    def _(b):
        departed(sent, b, sent_sem)
        departed(terms, b, terms_sem)


def on_device(tokens, norm_gains, qkv_weight, out_weight, up_weight, down_weight):
    arrays = (tokens, norm_gains, qkv_weight, out_weight, up_weight, down_weight)
    band = pltpu.VMEM((BANDS, BAND_TOKENS, CHANNELS), jnp.bfloat16)
    halves = pltpu.VMEM((2, BAND_TOKENS, 128), jnp.float32)
    twice = pl.pallas_call(
        kernel,
        out_shape=pltpu.VMEM(tokens.shape, jnp.bfloat16),
        in_specs=[pl.BlockSpec(memory_space=pl.ANY)] * 6,
        out_specs=pl.BlockSpec(memory_space=pltpu.VMEM),
        scratch_shapes=[pltpu.VMEM(a.shape, a.dtype) for a in arrays]
        + [band] * 4
        + [halves] * 2
        + [
            pltpu.SemaphoreType.DMA((BANDS,)),
            pltpu.SemaphoreType.DMA,
            pltpu.SemaphoreType.DMA((2, 4)),
        ]
        + [pltpu.SemaphoreType.DMA((BANDS,))] * 4,
        compiler_params=pltpu.CompilerParams(
            collective_id=0, has_side_effects=True, vmem_limit_bytes=60 * 2**20
        ),
    )(*arrays)
    return twice * 0.5


def solution(mesh):
    return jax.shard_map(
        on_device,
        mesh=mesh,
        in_specs=(P("rows", "cols", None), P(), P(), P(), P(), P()),
        out_specs=P("rows", "cols", None),
        check_vma=False,
    )
```

```python
import math

import jax
import jax.numpy as jnp
from jax import lax
from jax.experimental import pallas as pl
from jax.experimental.pallas import tpu as pltpu
from jax.sharding import PartitionSpec as P

HEADS = 8
EPSILON = 1e-06
CHANNELS = 256
HEAD_DIM = CHANNELS // HEADS
SCORE_SCALE = math.log2(math.e) / math.sqrt(HEAD_DIM)
BANDS = 4
BAND_ROWS = 8
BREADTH = 128
BAND_TOKENS = BAND_ROWS * BREADTH
PEERS = 64
CHUNK = BAND_TOKENS // PEERS
WINDOW_STRAND = 512
GRID_STRAND = 512
FINAL_STRAND = 256
MESH = pl.DeviceIdType.MESH


def layer_norm(x, gain):
    centred = x - jnp.mean(x, axis=-1, keepdims=True)
    spread = jnp.mean(centred * centred, axis=-1, keepdims=True)
    return (centred * lax.rsqrt(spread + EPSILON) * gain).astype(jnp.bfloat16)


def dot(a, b):
    return jnp.dot(a, b, preferred_element_type=jnp.float32)


def interleave(strands):
    waiting, active = list(strands), []
    while waiting or active:
        if waiting:
            active.append(waiting.pop(0))
        for strand in list(active):
            if next(strand, strand) is strand:
                active.remove(strand)


def feed_forward(mix, gain, up, down):
    normed = layer_norm(mix, gain)
    yield
    twice = []
    for c in range(0, up.shape[1], 512):
        units = dot(normed, up[:, c : c + 512])
        twice.append((units + units * lax.erf(units * math.sqrt(0.5))).astype(jnp.bfloat16))
        yield
    return (mix + mix) + dot(jnp.concatenate(twice, axis=1), down[...])


def spread_heads(x, masks):
    zero = jnp.zeros((16, 128), x.dtype)
    rows = []
    for t in range(4):
        low, high = x[16 * t : 16 * t + 16, :128], x[16 * t : 16 * t + 16, 128:]
        rows += [jnp.concatenate([low * m, zero], axis=1) for m in masks]
        rows += [jnp.concatenate([zero, high * m], axis=1) for m in masks]
    return jnp.concatenate(rows, axis=0)


def segment_max(x, lane, d=8):
    if d == 0:
        return x
    half = x.shape[0] // 2
    a, b = x[:half], x[half:]
    first = (lane & d) == 0
    both = jnp.where(
        first,
        jnp.maximum(a, pltpu.roll(a, 128 - d, 1)),
        jnp.maximum(b, pltpu.roll(b, d, 1)),
    )
    both = segment_max(both, lane, d // 2)
    return jnp.concatenate(
        [jnp.where(first, both, pltpu.roll(both, d, 1)), jnp.where(first, pltpu.roll(both, 128 - d, 1), both)],
        axis=0,
    )


def attention(normed, qkv_weight, out_weight, masks, ones, lane):
    qkv = dot(normed, qkv_weight[...]).astype(jnp.bfloat16)
    yield
    groups = [slice(64 * w, 64 * w + 64) for w in range(normed.shape[0] // 64)]
    scores = [
        lax.dot_general(
            qkv[g, :CHANNELS],
            spread_heads(qkv[g, CHANNELS : 2 * CHANNELS], masks),
            (((1,), (1,)), ((), ())),
            preferred_element_type=jnp.float32,
        )
        for g in groups
    ]
    scores = jnp.concatenate(scores, axis=0)
    parts = [scores[:, 128 * t : 128 * t + 128] for t in range(4)]
    top = jnp.maximum(jnp.maximum(parts[0], parts[1]), jnp.maximum(parts[2], parts[3]))
    yield
    top = segment_max(top, lane)
    yield
    weights = [jnp.exp2((p - top) * SCORE_SCALE) for p in parts]
    total = (weights[0] + weights[1]) + (weights[2] + weights[3])
    coarse = total.astype(jnp.bfloat16)
    fine = (total - coarse.astype(jnp.float32)).astype(jnp.bfloat16)
    weights = jnp.concatenate([w.astype(jnp.bfloat16) for w in weights], axis=1)
    yield
    total = dot(jnp.concatenate([coarse, fine], axis=1), ones)
    mixed = [
        dot(weights[g], spread_heads(qkv[g, 2 * CHANNELS :], masks)) for g in groups
    ]
    mixed = (jnp.concatenate(mixed, axis=0) / total).astype(jnp.bfloat16)
    yield
    return dot(mixed, out_weight[...])


def kernel(
    tokens_hbm, gains_hbm, qkv_hbm, out_hbm, up_hbm, down_hbm, result,
    tokens, gains, qkv_weight, out_weight, up_weight, down_weight,
    sent, recv, terms, back, regroup, ungroup,
    token_sem, gain_sem, weight_sem, sent_sem, recv_sem, terms_sem, back_sem,
):
    row, col = lax.axis_index("rows"), lax.axis_index("cols")
    core, place_row = lax.rem(row, 2), lax.div(row, 2)
    me = place_row * 8 + col

    def load_tokens(b):
        rows = pl.ds(b * BAND_ROWS, BAND_ROWS)
        return pltpu.make_async_copy(tokens_hbm.at[rows], tokens.at[rows], token_sem.at[b])

    def load_weights(i):
        pairs = ((qkv_hbm, qkv_weight), (out_hbm, out_weight), (up_hbm, up_weight), (down_hbm, down_weight))
        return [
            pltpu.make_async_copy(src.at[i], dst.at[i], weight_sem.at[i, n])
            for n, (src, dst) in enumerate(pairs)
        ]

    load_gains = pltpu.make_async_copy(gains_hbm, gains, gain_sem)
    load_gains.start()
    load_tokens(0).start()
    for copy in load_weights(0):
        copy.start()
    peer_cols = [lax.rem(col + c, 8) for c in range(8)]

    def each_peer(act):
        for a in range(8):
            r = lax.rem(place_row + a, 8)
            for c in range(8):
                if a + c > 0:
                    act(r * 8 + peer_cols[c], (2 * r + core, peer_cols[c]))

    barrier = pltpu.get_barrier_semaphore()
    each_peer(
        lambda p, device: pl.semaphore_signal(barrier, inc=1, device_id=device, device_id_type=MESH)
    )

    def chunk(ref, b, p):
        return ref.at[b, pl.ds(pl.multiple_of(p * CHUNK, CHUNK), CHUNK)]

    def exchange(src, dst, b, src_sem, dst_sem):
        each_peer(
            lambda p, device: pltpu.make_async_remote_copy(
                src_ref=chunk(src, b, p), dst_ref=chunk(dst, b, me),
                send_sem=src_sem.at[b], recv_sem=dst_sem.at[b],
                device_id=device, device_id_type=MESH,
            ).start()
        )
        own = pl.ds(pl.multiple_of(me * CHUNK, CHUNK), CHUNK)
        dst[b, own, :] = src[b, own, :]

    def arrived(dst, b, dst_sem):
        part = dst.at[b, pl.ds(0, (PEERS - 1) * CHUNK)]
        pltpu.make_async_copy(part, part, dst_sem.at[b]).wait()

    def departed(src, b, src_sem):
        part = src.at[b, pl.ds(0, (PEERS - 1) * CHUNK)]
        pltpu.make_async_copy(part, part, src_sem.at[b]).wait()

    channel = lax.broadcasted_iota(jnp.int32, (1, 128), 1)
    masks = [(channel // HEAD_DIM == j).astype(jnp.bfloat16) for j in range(4)]
    key_head = lax.broadcasted_iota(jnp.int32, (CHANNELS, CHANNELS), 0) // 16 % HEADS
    channel_head = lax.broadcasted_iota(jnp.int32, (CHANNELS, CHANNELS), 1) // HEAD_DIM
    ones = (key_head == channel_head).astype(jnp.bfloat16)
    lane = lax.broadcasted_iota(jnp.int32, (1, 128), 1)

    def window_strand(b, first):
        pairs = range(first // 128, (first + WINDOW_STRAND) // 128)
        x = []
        for p in pairs:
            strips = [
                tokens[b * BAND_ROWS + r, 16 * p : 16 * p + 16, :].astype(jnp.float32) for r in range(8)
            ]
            x += [s[:8] for s in strips] + [s[8:] for s in strips]
        x = jnp.concatenate(x, axis=0)
        normed = layer_norm(x, gains[0:1])
        yield
        terms_a = yield from attention(normed, qkv_weight.at[0], out_weight.at[0], masks, ones, lane)
        mixed = (x + terms_a).astype(jnp.bfloat16).astype(jnp.float32)
        yield
        y = yield from feed_forward(mixed, gains[1:2], up_weight.at[0], down_weight.at[0])
        for n, p in enumerate(pairs):
            for r in range(8):
                lo, hi = 128 * n + 8 * r, 128 * n + 64 + 8 * r
                strip = 0.5 * jnp.concatenate([y[lo : lo + 8], y[hi : hi + 8]], axis=0)
                sent[b, 128 * r + 16 * p : 128 * r + 16 * p + 16, :] = strip.astype(jnp.bfloat16)

    def grid_strand(first):
        members = range(first // 64, (first + GRID_STRAND) // 64)
        x = jnp.concatenate(
            [
                jnp.concatenate([regroup[h, pl.ds(g, 64, stride=CHUNK), :] for h in range(2)], axis=1)
                for g in members
            ],
            axis=0,
        )
        normed = layer_norm(x, gains[2:3])
        yield
        y = yield from attention(normed, qkv_weight.at[1], out_weight.at[1], masks, ones, lane)
        for n, g in enumerate(members):
            for h in range(2):
                ungroup[h, pl.ds(g, 64, stride=CHUNK), :] = y[
                    64 * n : 64 * n + 64, 128 * h : 128 * h + 128
                ]

    def final_strand(b, first):
        span = pl.ds(first, FINAL_STRAND)
        mixed = sent[b, span, :].astype(jnp.float32) + back[b, span, :].astype(jnp.float32)
        mixed = mixed.astype(jnp.bfloat16).astype(jnp.float32)
        yield
        y = yield from feed_forward(mixed, gains[3:4], up_weight.at[1], down_weight.at[1])
        rows = FINAL_STRAND // BREADTH
        result[pl.ds(b * BAND_ROWS + first // BREADTH, rows), :, :] = y.astype(jnp.bfloat16).reshape(
            rows, BREADTH, CHANNELS
        )

    @pl.loop(0, BANDS + 5)
    def _(t):
        @pl.when(t == 0)
        def _():
            load_gains.wait()
            for copy in load_weights(0):
                copy.wait()
            for b in range(1, BANDS):
                load_tokens(b).start()
            for copy in load_weights(1):
                copy.start()

        @pl.when(t < BANDS)
        def _():
            load_tokens(t).wait()
            interleave(window_strand(t, f) for f in range(0, BAND_TOKENS, WINDOW_STRAND))

        @pl.when(t == 0)
        def _():
            pl.semaphore_wait(barrier, PEERS - 1)
            for copy in load_weights(1):
                copy.wait()

        @pl.when(t < BANDS)
        def _():
            exchange(sent, recv, t, sent_sem, recv_sem)

        @pl.when((t == 1) | ((t >= 3) & (t < BANDS + 2)))
        def _():
            b = jnp.where(t < 2, 0, t - 2)
            arrived(recv, b, recv_sem)
            for h in range(2):
                regroup[h] = recv[b, :, 128 * h : 128 * h + 128].astype(jnp.float32)
            interleave(grid_strand(f) for f in range(0, BAND_TOKENS, GRID_STRAND))
            for h in range(2):
                terms[b, :, 128 * h : 128 * h + 128] = ungroup[h].astype(jnp.bfloat16)
            exchange(terms, back, b, terms_sem, back_sem)

        @pl.when(t >= 5)
        def _():
            b = t - 5
            arrived(back, b, back_sem)
            interleave(final_strand(b, f) for f in range(0, BAND_TOKENS, FINAL_STRAND))

    @pl.loop(0, BANDS)
    def _(b):
        departed(sent, b, sent_sem)
        departed(terms, b, terms_sem)


def on_device(tokens, norm_gains, qkv_weight, out_weight, up_weight, down_weight):
    arrays = (tokens, norm_gains, qkv_weight, out_weight, up_weight, down_weight)
    band = pltpu.VMEM((BANDS, BAND_TOKENS, CHANNELS), jnp.bfloat16)
    halves = pltpu.VMEM((2, BAND_TOKENS, 128), jnp.float32)
    twice = pl.pallas_call(
        kernel,
        out_shape=pltpu.VMEM(tokens.shape, jnp.bfloat16),
        in_specs=[pl.BlockSpec(memory_space=pl.ANY)] * 6,
        out_specs=pl.BlockSpec(memory_space=pltpu.VMEM),
        scratch_shapes=[pltpu.VMEM(a.shape, a.dtype) for a in arrays]
        + [band] * 4
        + [halves] * 2
        + [
            pltpu.SemaphoreType.DMA((BANDS,)),
            pltpu.SemaphoreType.DMA,
            pltpu.SemaphoreType.DMA((2, 4)),
        ]
        + [pltpu.SemaphoreType.DMA((BANDS,))] * 4,
        compiler_params=pltpu.CompilerParams(
            collective_id=0, has_side_effects=True, vmem_limit_bytes=60 * 2**20
        ),
    )(*arrays)
    return twice * 0.5


def solution(mesh):
    return jax.shard_map(
        on_device,
        mesh=mesh,
        in_specs=(P("rows", "cols", None), P(), P(), P(), P(), P()),
        out_specs=P("rows", "cols", None),
        check_vma=False,
    )
```
